256 devices in a mesh: tm: 32 (over z_hi, y, core), seq: 8 (over x, z_lo).
Axes of the slice: x: 4, y: 4, z: 8 (z_hi: 4, z_lo: 2; z = z_hi * 2 + z_lo), core: 2. Of those that a mesh axis runs over, the one named last changes fastest.
Arguments:
- projected: bfloat16 [32, 1024, 3, 3072], P('tm', 'seq'), may hold values from -32 to 32
- residual: bfloat16 [32, 1024, 3072], P('tm', 'seq'), may hold values from -3 to 3
- timesteps: int32 [32], P('tm'), may hold values from 0 to 49
- gate_table: float32 [50, 3072], replicated, may hold values from 0.2 to 2
- out_weight: bfloat16 [3072, 3072], P(('tm', 'seq')), may hold values from -0.4375 to 0.4375
Outputs:
- block_out: bfloat16 [32, 1024, 3072], P('tm', 'seq')
The draws below stay inside these ranges and needn't reach their ends.
All inputs are finite; a program needn't handle non-finite values.
Results may differ from the reference program's by a relative error of at most 0.0052.
Values may be sent and summed in bfloat16 or wider, within the bound.
A program may use at most 128 MiB of HBM per device.

```python
import math
import jax
import jax.numpy as jnp
from jax import lax

HEADS = 24
HEAD_DIM = 128
DOUT = 3072
NSTEPS = 50
SEQ = 1024
BLOCKS = 32


def draw_projected(key, part):
    key = jax.random.fold_in(key, 7)
    shape = (BLOCKS, SEQ, 3, HEADS * HEAD_DIM)
    base = jnp.clip(1.5 * jax.random.normal(key, shape, jnp.float32), -6.0, 6.0)
    return base.astype(jnp.bfloat16)


def plant(drawn, key, low, high):
    place = [jax.random.randint(jax.random.fold_in(key, axis), (), 0, length) for axis, length in enumerate(drawn.shape)]
    longest = drawn.shape.index(max(drawn.shape))
    neighbour = place[:longest] + [(place[longest] + 1) % drawn.shape[longest]] + place[longest + 1:]
    return drawn.at[tuple(place)].set(low).at[tuple(neighbour)].set(high)


def block_scale(own_key, dims, split, low, high):
    def one(dim, blocks):
        steps = jax.random.uniform(jax.random.fold_in(jax.random.fold_in(own_key, 6), dim), (blocks,), jnp.float32, low / len(split), high / len(split))
        return jnp.repeat(jnp.exp(steps), dims[dim] // blocks).reshape((-1,) + (1,) * (len(dims) - dim - 1))

    factor_of = one(*split[0])
    for cut in split[1:]:
        factor_of = factor_of * one(*cut)
    return factor_of


def bell_draw(stream_key, shape, deviation, most, pieces=(), kind=jnp.bfloat16):
    level = block_scale(stream_key, shape, pieces, -0.22, 0.18) if pieces else 1.0
    drawn = jax.random.normal(stream_key, shape, jnp.float32) * deviation * level
    return jnp.minimum(jnp.maximum(drawn, -most), most).astype(kind)


def setup_inputs(seed: int = 0) -> dict:
    splits = jax.random.split(jax.random.key(seed), 6)
    projected = draw_projected(jax.random.fold_in(splits[5], 71), 0)
    residual = bell_draw(splits[1], (BLOCKS, SEQ, DOUT), 0.5, 3.0, ((0, 32), (1, 8)))
    timesteps = plant(jax.random.randint(splits[2], (BLOCKS,), 0, NSTEPS), jax.random.fold_in(splits[2], 1), 0, NSTEPS - 1).astype(jnp.int32)
    gate_table = jnp.clip(jax.random.uniform(splits[3], (NSTEPS, DOUT), jnp.float32, 0.2, 2.0), 0.2, 2.0)
    out_weight = bell_draw(splits[4], (HEADS * HEAD_DIM, DOUT), (HEADS * HEAD_DIM // 16) ** -0.5, 0.4375, ((0, 256),))
    return {"projected": projected, "residual": residual, "timesteps": timesteps, "gate_table": gate_table, "out_weight": out_weight}


def attend_block(block):
    queries = block[:, 0].reshape(SEQ, HEADS, HEAD_DIM).transpose(1, 0, 2)
    keys = block[:, 1].reshape(SEQ, HEADS, HEAD_DIM).transpose(1, 0, 2)
    values = block[:, 2].reshape(SEQ, HEADS, HEAD_DIM).transpose(1, 0, 2)
    scale = 1.0 / math.sqrt(HEAD_DIM)

    def one_head(triple):
        head_q, head_k, head_v = triple
        scores = jnp.dot(head_q, head_k.T, preferred_element_type=jnp.float32) * scale
        top = lax.optimization_barrier(jnp.max(scores, axis=-1, keepdims=True))
        weights = jnp.exp(scores - top)
        totals = lax.optimization_barrier(jnp.sum(weights, axis=-1, keepdims=True))
        probs = weights.astype(jnp.bfloat16)
        summed = jnp.dot(probs, head_v, preferred_element_type=jnp.float32)
        return (summed / totals).astype(jnp.bfloat16)
    heads_out = lax.map(one_head, (queries, keys, values))
    return heads_out.transpose(1, 0, 2).reshape(SEQ, HEADS * HEAD_DIM)

def reference(projected, residual, timesteps, gate_table, out_weight):

    def one_block(triple):
        block, resid, step = triple
        attended = attend_block(block)
        gate = gate_table[step]
        product = jnp.dot(attended, out_weight, preferred_element_type=jnp.float32)
        return (resid.astype(jnp.float32) + gate * product).astype(jnp.bfloat16)
    return lax.map(one_block, (projected, residual, timesteps))
```

```python
import functools
import math

import jax
import jax.numpy as jnp
from jax import lax
from jax.experimental import pallas as pl
from jax.experimental.pallas import tpu as pltpu
from jax.sharding import PartitionSpec as P

MESH = pl.DeviceIdType.MESH
HD = 128
NH = 3
NS = 8
TOK = 128
QCOLS = 768
ROWS = 96
QBLK = 256
NCOL = 256


def coords():
    tm, s = lax.axis_index("tm"), lax.axis_index("seq")
    core = lax.rem(tm, 2)
    y = lax.rem(lax.div(tm, 2), 4)
    z = lax.div(tm, 8) * 2 + lax.rem(s, 2)
    return lax.div(s, 2), y, z, core


def device(x, y, z, core):
    return (lax.div(z, 2) * 8 + y * 2 + core, x * 2 + lax.rem(z, 2))


def kernel(
    proj, w_ref, out_ref,
    qkv, held, att, wpad, raw, wbuf, prod,
    first_send, first_recv, qkv_send, qkv_recv, z_send, z_recv, y_send, y_recv,
    relay_send, relay_recv, att_send, att_recv, pair_send, pair_recv, ret_send, ret_recv,
):
    x, y, z, core = coords()
    s = lax.axis_index("seq")
    zl = lax.rem(z, 2)
    zbase = z - zl
    twin = 1 - core
    xbit = lax.rem(x, 2)
    xother = x + 1 - 2 * xbit
    up = lax.rem(y + 1, 4)
    down = lax.rem(y + 3, 4)
    zup = lax.rem(z + 1, 8)
    zdown = lax.rem(z + 7, 8)

    def remote(src, dst, send, recv, target):
        return pltpu.make_async_remote_copy(
            src_ref=src, dst_ref=dst, send_sem=send, recv_sem=recv,
            device_id=target, device_id_type=MESH,
        )

    barrier = pltpu.get_barrier_semaphore()
    peers = []
    for c in (core, twin):
        for d in range(NS):
            if c is core and d == 0:
                continue
            other = lax.rem(s + d, NS)
            peers.append(device(lax.div(other, 2), y, zbase + lax.rem(other, 2), c))
    zouter = lax.rem(z + 7 + 2 * zl, 8)
    peers.append(device(x, y, zouter, core))
    peers.append(device(x, up, z, core))
    peers.append(device(x, down, z, core))
    for peer in peers:
        pl.semaphore_signal(barrier, inc=1, device_id=peer, device_id_type=MESH)

    wpad[...] = jnp.zeros_like(wpad)
    wpad[0:12, :] = w_ref[...]
    pl.semaphore_wait(barrier, len(peers))

    for k in range(NS):
        xt, ct = k // 2, k % 2
        quarter = (xt % 2) * 2 + ct
        src = wpad.at[:, pl.ds(quarter * QCOLS, QCOLS)]
        own = (x == xt) & (core == ct) & (zl == core)

        @pl.when(own)
        def _():
            pltpu.make_async_copy(src, raw.at[s], first_recv.at[s]).start()

        @pl.when(jnp.logical_not(own))
        def _():
            remote(
                src, raw.at[s], first_send.at[k], first_recv.at[s],
                device(jnp.int32(xt), y, zbase + core, jnp.int32(ct)),
            ).start()

    def qkv_copy(h, d):
        other = lax.rem(s + d, NS)
        col = pl.multiple_of((NS * h + other) * HD, HD)
        src = proj.at[:, :, pl.ds(col, HD)]
        dst = qkv.at[h, :, pl.ds(pl.multiple_of(s * TOK, TOK), TOK), :]
        if d == 0:
            return pltpu.make_async_copy(src, dst, qkv_recv.at[h])
        target = device(lax.div(other, 2), y, zbase + lax.rem(other, 2), core)
        return remote(src, dst, qkv_send.at[h * NS + d], qkv_recv.at[h], target)

    for h in range(NH):
        for d in range(NS):
            qkv_copy(h, d).start()

    for k in range(NS):
        pltpu.make_async_copy(raw.at[k], raw.at[k], first_recv.at[k]).wait()
    row = lax.broadcasted_iota(jnp.int32, (ROWS, 128), 0)
    col = lax.broadcasted_iota(jnp.int32, (ROWS, 128), 1)
    piece = lax.div(row, 12)
    pick = (col == piece * 16 + (row - piece * 12)).astype(jnp.float32).astype(jnp.bfloat16)
    tile = jnp.dot(
        pick, raw[...].reshape(128, QCOLS), preferred_element_type=jnp.float32
    ).astype(jnp.bfloat16)

    def tile_row(ty, tz):
        return pl.multiple_of((lax.div(tz, 2) * 8 + ty * 2 + lax.rem(tz, 2)) * ROWS, 32)

    wbuf[pl.ds(tile_row(y, z), ROWS), :] = tile

    order = [0, -1, 1, -2, 2, -3, 3, -4]

    def slot(ty, off, lo=0, n=ROWS):
        return wbuf.at[pl.ds(pl.multiple_of(tile_row(ty, lax.rem(z + off + 8, 8)) + lo, 16), n), :]

    def z_copy(off_at_sender):
        going_up, hops = off_at_sender
        off = -hops if going_up else hops
        ref = slot(y, off)
        k = hops if going_up else 4 + hops
        return remote(
            ref, ref, z_send.at[k], z_recv.at[k],
            device(x, y, zup if going_up else zdown, core),
        )

    def z_wait(going_up, hops):
        ref = slot(y, -(hops + 1) if going_up else hops + 1)
        k = hops if going_up else 4 + hops
        pltpu.make_async_copy(ref, ref, z_recv.at[k]).wait()

    def y_copy(i, going_up):
        ref = slot(y, order[i])
        k = 2 * i + (0 if going_up else 1)
        return remote(
            ref, ref, y_send.at[k], y_recv.at[k], device(x, up if going_up else down, z, core)
        )

    def relay_copy(i, going_up):
        ref = slot(down if going_up else up, order[i], 0 if going_up else 48, 48)
        k = 2 * i + (0 if going_up else 1)
        return remote(
            ref, ref, relay_send.at[k], relay_recv.at[k],
            device(x, up if going_up else down, z, core),
        )

    def share(i):
        y_copy(i, True).start()
        y_copy(i, False).start()

    def relay(i):
        for going_up in (True, False):
            ref = slot(down if going_up else up, order[i])
            pltpu.make_async_copy(ref, ref, y_recv.at[2 * i + (0 if going_up else 1)]).wait()
            relay_copy(i, going_up).start()

    def z_step(hops):
        z_wait(True, hops - 1)
        if hops < 4:
            z_copy((True, hops)).start()
        share(2 * hops - 1)
        if hops < 4:
            z_wait(False, hops - 1)
            if hops < 3:
                z_copy((False, hops)).start()
            share(2 * hops)

    z_copy((True, 0)).start()
    z_copy((False, 0)).start()
    share(0)

    def attend(h):
        ref = qkv.at[h]
        pltpu.make_async_copy(ref, ref, qkv_recv.at[h]).wait()
        factor = math.log2(math.e) / math.sqrt(HD)

        @pl.loop(0, NS * TOK // QBLK)
        def _(i):
            q = qkv[h, 0, pl.ds(pl.multiple_of(i * QBLK, QBLK), QBLK), :]
            scores = lax.dot_general(
                q, qkv[h, 1], (((1,), (1,)), ((), ())), preferred_element_type=jnp.float32
            ) * factor
            weights = jnp.exp2(scores - jnp.max(scores, axis=1, keepdims=True))
            totals = jnp.sum(weights, axis=1, keepdims=True)
            summed = jnp.dot(
                weights.astype(jnp.bfloat16), qkv[h, 2], preferred_element_type=jnp.float32
            )
            res = (summed / totals).astype(jnp.bfloat16).reshape(1, 1, 2, TOK, HD)
            held[pl.ds(h, 1), pl.ds(lax.div(i, 2), 1), pl.ds(lax.rem(i, 2), 1)] = res[None]

        for d in range(NS):
            att_copy(h, d).start()

    def att_copy(h, d):
        other = lax.rem(s + d, NS)
        src = held.at[h, lax.div(other, 4), :, lax.rem(other, 2)]
        dst = att.at[h, core, :, :, pl.ds(pl.multiple_of(s * HD, HD), HD)]
        if d == 0:
            return pltpu.make_async_copy(src, dst, att_recv.at[h])
        target = device(lax.div(other, 2), y, zbase + lax.rem(other, 2), core)
        return remote(src, dst, att_send.at[h * NS + d], att_recv.at[h], target)

    def pair_copy(h):
        ref = att.at[h, core]
        return remote(ref, ref, pair_send.at[h], pair_recv.at[h], device(x, y, z, twin))

    def pair(h):
        ref = att.at[h, core]
        pltpu.make_async_copy(ref, ref, att_recv.at[h]).wait()
        pair_copy(h).start()

    z_step(1)
    relay(0)
    attend(0)
    z_step(2)
    relay(1)
    relay(2)
    attend(1)
    pair(0)
    z_step(3)
    z_step(4)
    relay(3)
    relay(4)
    attend(2)
    pair(1)
    relay(5)
    relay(6)
    pair(2)
    relay(7)
    for i in range(8):
        for going_up in (True, False):
            ref = slot(lax.rem(y + 2, 4), order[i], 0 if going_up else 48, 48)
            pltpu.make_async_copy(ref, ref, relay_recv.at[2 * i + (0 if going_up else 1)]).wait()
    for h in range(NH):
        ref = att.at[h, twin]
        pltpu.make_async_copy(ref, ref, pair_recv.at[h]).wait()

    quarter = (xbit * 2 + core) * QCOLS

    def product(bit, n):
        total = None
        for h in range(NH):
            left = att[h, :, pl.ds(bit, 1)].reshape(2 * TOK, NS * HD)
            term = jnp.dot(
                left, wbuf[h * NS * HD:(h + 1) * NS * HD, n * NCOL:(n + 1) * NCOL],
                preferred_element_type=jnp.float32,
            )
            total = term if total is None else total + term
        return total.astype(jnp.bfloat16).reshape(2, 1, TOK, NCOL)

    def ret_copy(n, blk, far):
        cols = pl.ds(n * NCOL, NCOL)
        to = pl.ds(pl.multiple_of(quarter + n * NCOL, NCOL), NCOL)
        src = prod.at[blk, (1 - xbit) if far else xbit, :, cols]
        dst = out_ref.at[:, to]
        k = (0 if blk is core else 1) + (0 if far else 2)
        if not far and blk is core:
            return pltpu.make_async_copy(src, dst, ret_recv.at[k * 3 + n])
        return remote(
            src, dst, ret_send.at[k * 3 + n], ret_recv.at[k * 3 + n],
            device(xother if far else x, y, z, blk),
        )

    for far in (True, False):
        bit = 1 - xbit if far else xbit
        for n in range(QCOLS // NCOL):
            prod[:, pl.ds(bit, 1), :, n * NCOL:(n + 1) * NCOL] = product(bit, n)
            for blk in (core, twin):
                ret_copy(n, blk, far).start()

    for n in range(QCOLS // NCOL):
        for far in (True, False):
            for blk in (core, twin):
                c = ret_copy(n, blk, far)
                if far or blk is twin:
                    c.wait_send()
        for far in (True, False):
            for blk in (core, twin):
                k = (0 if blk is core else 1) + (0 if far else 2)
                fq = ((1 - xbit if far else xbit) * 2 + blk) * QCOLS + n * NCOL
                ref = out_ref.at[:, pl.ds(pl.multiple_of(fq, NCOL), NCOL)]
                pltpu.make_async_copy(ref, ref, ret_recv.at[k * 3 + n]).wait()
    for k in range(NS):
        own = (x == k // 2) & (core == k % 2) & (zl == core)

        @pl.when(jnp.logical_not(own))
        def _():
            remote(
                wpad.at[:, pl.ds(0, QCOLS)], raw.at[s], first_send.at[k], first_recv.at[s],
                device(jnp.int32(k // 2), y, zbase + core, jnp.int32(k % 2)),
            ).wait_send()

    for h in range(NH):
        for d in range(1, NS):
            qkv_copy(h, d).wait_send()
            att_copy(h, d).wait_send()
        pair_copy(h).wait_send()
    for hops in range(4):
        z_copy((True, hops)).wait_send()
        if hops < 3:
            z_copy((False, hops)).wait_send()
    for i in range(8):
        for going_up in (True, False):
            y_copy(i, going_up).wait_send()
            relay_copy(i, going_up).wait_send()


def project(proj, w):
    bf = jnp.bfloat16
    dma = pltpu.SemaphoreType.DMA
    return pl.pallas_call(
        kernel,
        out_shape=jax.ShapeDtypeStruct((TOK, 4 * QCOLS), bf),
        in_specs=[pl.BlockSpec(memory_space=pl.ANY), pl.BlockSpec(memory_space=pltpu.VMEM)],
        out_specs=pl.BlockSpec(memory_space=pltpu.VMEM),
        scratch_shapes=[
            pltpu.VMEM((NH, 3, NS * TOK, HD), bf),
            pltpu.VMEM((NH, 2, 2, 2, TOK, HD), bf),
            pltpu.VMEM((NH, 2, 2, TOK, NS * HD), bf),
            pltpu.VMEM((16, 4 * QCOLS), bf),
            pltpu.VMEM((NS, 16, QCOLS), bf),
            pltpu.VMEM((32 * ROWS, QCOLS), bf),
            pltpu.VMEM((2, 2, TOK, QCOLS), bf),
            dma((NS,)), dma((NS,)),
            dma((NH * NS,)), dma((NH,)),
            dma((7,)), dma((7,)),
            dma((16,)), dma((16,)),
            dma((16,)), dma((16,)),
            dma((NH * NS,)), dma((NH,)),
            dma((NH,)), dma((NH,)),
            dma((12,)), dma((12,)),
        ],
        compiler_params=pltpu.CompilerParams(
            collective_id=0, has_side_effects=True, vmem_limit_bytes=40 << 20
        ),
        name="attend_project",
    )(proj, w)


def shards(projected, residual, timesteps, gate_table, out_weight):
    product = project(projected[0].transpose(1, 0, 2), out_weight)
    gate = lax.dynamic_slice(gate_table, (timesteps[0], 0), (1, gate_table.shape[1]))
    result = residual[0].astype(jnp.float32) + gate * product.astype(jnp.float32)
    return result.astype(jnp.bfloat16)[None]


def solution(mesh):
    placed = (
        P("tm", "seq", None, None),
        P("tm", "seq", None),
        P("tm"),
        P(),
        P(("tm", "seq"), None),
    )
    return jax.shard_map(
        shards, mesh=mesh, in_specs=placed, out_specs=P("tm", "seq", None), check_vma=False
    )
```

```python
import functools
import math

import jax
import jax.numpy as jnp
from jax import lax
from jax.experimental import pallas as pl
from jax.experimental.pallas import tpu as pltpu
from jax.sharding import PartitionSpec as P

MESH = pl.DeviceIdType.MESH
HD = 128
NH = 3
NS = 8
TOK = 128
QCOLS = 768
ROWS = 96
QBLK = 256
NCOL = 256


def coords():
    tm, s = lax.axis_index("tm"), lax.axis_index("seq")
    core = lax.rem(tm, 2)
    y = lax.rem(lax.div(tm, 2), 4)
    z = lax.div(tm, 8) * 2 + lax.rem(s, 2)
    return lax.div(s, 2), y, z, core


def device(x, y, z, core):
    return (lax.div(z, 2) * 8 + y * 2 + core, x * 2 + lax.rem(z, 2))


def kernel(
    proj, w_ref, out_ref,
    qkv, held, att, wpad, raw, wbuf, prod,
    first_send, first_recv, qkv_send, qkv_recv, z_send, z_recv, y_send, y_recv,
    relay_send, relay_recv, att_send, att_recv, cross_send, cross_recv, hand_send, hand_recv,
    last_send, last_recv, last_pair_send, last_pair_recv, pair_send, pair_recv, ret_send, ret_recv,
    wown, load_sem, acc,
):
    x, y, z, core = coords()
    s = lax.axis_index("seq")
    zl = lax.rem(z, 2)
    zbase = z - zl
    twin = 1 - core
    xbit = lax.rem(x, 2)
    xother = x + 1 - 2 * xbit
    up = lax.rem(y + 1, 4)
    down = lax.rem(y + 3, 4)
    zup = lax.rem(z + 1, 8)
    zdown = lax.rem(z + 7, 8)

    def remote(src, dst, send, recv, target):
        return pltpu.make_async_remote_copy(
            src_ref=src, dst_ref=dst, send_sem=send, recv_sem=recv,
            device_id=target, device_id_type=MESH,
        )

    barrier = pltpu.get_barrier_semaphore()
    peers = []
    for c in (core, twin):
        for d in range(NS):
            if c is core and d == 0:
                continue
            other = lax.rem(s + d, NS)
            peers.append(device(lax.div(other, 2), y, zbase + lax.rem(other, 2), c))
    zouter = lax.rem(z + 7 + 2 * zl, 8)
    peers.append(device(x, y, zouter, core))
    peers.append(device(x, up, z, core))
    peers.append(device(x, down, z, core))
    for peer in peers:
        pl.semaphore_signal(barrier, inc=1, device_id=peer, device_id_type=MESH)

    load = pltpu.make_async_copy(w_ref, wown, load_sem)
    load.start()
    wpad[...] = jnp.zeros_like(wpad)
    load.wait()
    wpad[0:12, :] = wown[...]
    pl.semaphore_wait(barrier, len(peers))

    for k in range(NS):
        xt, ct = k // 2, k % 2
        quarter = (xt % 2) * 2 + ct
        src = wpad.at[:, pl.ds(quarter * QCOLS, QCOLS)]
        own = (x == xt) & (core == ct) & (zl == core)

        @pl.when(own)
        def _():
            pltpu.make_async_copy(src, raw.at[s], first_recv.at[s]).start()

        @pl.when(jnp.logical_not(own))
        def _():
            remote(
                src, raw.at[s], first_send.at[k], first_recv.at[s],
                device(jnp.int32(xt), y, zbase + core, jnp.int32(ct)),
            ).start()

    def qkv_copy(h, d):
        other = lax.rem(s + d, NS)
        col = pl.multiple_of((NS * h + other) * HD, HD)
        src = proj.at[:, :, pl.ds(col, HD)]
        dst = qkv.at[h, :, pl.ds(pl.multiple_of(s * TOK, TOK), TOK), :]
        if d == 0:
            return pltpu.make_async_copy(src, dst, qkv_recv.at[h])
        target = device(lax.div(other, 2), y, zbase + lax.rem(other, 2), core)
        return remote(src, dst, qkv_send.at[h * NS + d], qkv_recv.at[h], target)

    def same(h):
        for d in (2, 6, 4, 0):
            qkv_copy(h, d).start()

    def other(h):
        for d in (1, 7, 3, 5):
            qkv_copy(h, d).start()

    other(0)
    same(0)
    same(1)
    for k in range(NS):
        pltpu.make_async_copy(raw.at[k], raw.at[k], first_recv.at[k]).wait()
    row = lax.broadcasted_iota(jnp.int32, (ROWS, 128), 0)
    col = lax.broadcasted_iota(jnp.int32, (ROWS, 128), 1)
    piece = lax.div(row, 12)
    pick = (col == piece * 16 + (row - piece * 12)).astype(jnp.float32).astype(jnp.bfloat16)
    tile = jnp.dot(
        pick, raw[...].reshape(128, QCOLS), preferred_element_type=jnp.float32
    ).astype(jnp.bfloat16)

    def tile_row(ty, tz):
        return pl.multiple_of((lax.div(tz, 2) * 8 + ty * 2 + lax.rem(tz, 2)) * ROWS, 32)

    wbuf[pl.ds(tile_row(y, z), ROWS), :] = tile

    order = [0, -1, 1, -2, 2, -3, 3, -4]

    def slot(ty, off, lo=0, n=ROWS):
        first = tile_row(ty, lax.rem(z + off + 8, 8)) + lo
        return wbuf.at[pl.ds(pl.multiple_of(first, 16), n), :]

    def z_copy(going_up, hops):
        ref = slot(y, -hops if going_up else hops)
        k = (hops if going_up else 4 + hops)
        return remote(
            ref, ref, z_send.at[k], z_recv.at[k],
            device(x, y, zup if going_up else zdown, core),
        )

    def z_wait(going_up, hops):
        ref = slot(y, -(hops + 1) if going_up else hops + 1)
        k = (hops if going_up else 4 + hops)
        pltpu.make_async_copy(ref, ref, z_recv.at[k]).wait()

    def y_copy(i, going_up):
        ref = slot(y, order[i])
        k = 2 * i + (0 if going_up else 1)
        return remote(
            ref, ref, y_send.at[k], y_recv.at[k], device(x, up if going_up else down, z, core)
        )

    def relay_copy(i, going_up):
        ref = slot(down if going_up else up, order[i], 0 if going_up else 48, 48)
        k = 2 * i + (0 if going_up else 1)
        return remote(
            ref, ref, relay_send.at[k], relay_recv.at[k],
            device(x, up if going_up else down, z, core),
        )

    def share(i):
        y_copy(i, True).start()
        y_copy(i, False).start()

    def relay(*which):
        for i in which:
            for going_up in (True, False):
                ref = slot(down if going_up else up, order[i])
                k = 2 * i + (0 if going_up else 1)
                pltpu.make_async_copy(ref, ref, y_recv.at[k]).wait()
                relay_copy(i, going_up).start()

    def relayed():
        for i in range(8):
            for going_up in (True, False):
                ref = slot(lax.rem(y + 2, 4), order[i], 0 if going_up else 48, 48)
                k = 2 * i + (0 if going_up else 1)
                pltpu.make_async_copy(ref, ref, relay_recv.at[k]).wait()

    def z_step(hops):
        z_wait(True, hops - 1)
        if hops < 4:
            z_copy(True, hops).start()
        share(2 * hops - 1)
        if hops < 4:
            z_wait(False, hops - 1)
            if hops < 3:
                z_copy(False, hops).start()
            share(2 * hops)

    def z_first():
        z_copy(True, 0).start()
        z_copy(False, 0).start()
        share(0)

    z_first()
    other(1)
    same(2)

    last = NH - 1

    def attend(h):
        ref = qkv.at[h]
        pltpu.make_async_copy(ref, ref, qkv_recv.at[h]).wait()
        factor = math.log2(math.e) / math.sqrt(HD)

        @pl.loop(0, NS * TOK // QBLK)
        def _(i):
            q = qkv[h, 0, pl.ds(pl.multiple_of(i * QBLK, QBLK), QBLK), :]
            scores = lax.dot_general(
                q, qkv[h, 1], (((1,), (1,)), ((), ())), preferred_element_type=jnp.float32
            ) * factor
            weights = jnp.exp2(scores - jnp.max(scores, axis=1, keepdims=True))
            totals = jnp.sum(weights, axis=1, keepdims=True)
            summed = jnp.dot(
                weights.astype(jnp.bfloat16), qkv[h, 2], preferred_element_type=jnp.float32
            )
            res = (summed / totals).astype(jnp.bfloat16).reshape(1, 1, 2, TOK, HD)
            held[pl.ds(h, 1), pl.ds(lax.div(i, 2), 1), pl.ds(lax.rem(i, 2), 1)] = res[None]

        if h < last:
            for k in (0, 1):
                cross_copy(h, k).start()
            for k in (1, 3, 2, 0):
                own_copy(h, k).start()
        else:
            for far in (True, False):
                for d in (1, 7, 3, 5, 2, 6, 4, 0):
                    piece_copy(d, far).start()

    mine = pl.ds(pl.multiple_of(s * HD, HD), HD)

    def own_copy(h, k):
        xt = lax.rem(x + k, 4)
        src = held.at[h, lax.div(xt, 2), :, zl]
        dst = att.at[h, core, :, :, mine]
        if k == 0:
            return pltpu.make_async_copy(src, dst, att_recv.at[h])
        return remote(src, dst, att_send.at[h * 4 + k], att_recv.at[h], device(xt, y, z, core))

    def cross_copy(h, k):
        xt = x if k == 0 else 3 - x
        src = held.at[h, lax.div(xt, 2), :, 1 - zl]
        dst = att.at[h, core, :, :, mine]
        return remote(
            src, dst, cross_send.at[h * 2 + k], cross_recv.at[h],
            device(xt, y, zbase + 1 - zl, core),
        )

    def hand_copy(h, k):
        xt = x if k == 0 else 3 - x
        cols = pl.ds(pl.multiple_of((xt * 2 + 1 - zl) * HD, HD), HD)
        ref = att.at[h, core, :, :, cols]
        return remote(
            ref, ref, hand_send.at[h * 2 + k], hand_recv.at[h], device(xother, y, z, core)
        )

    def hand(h):
        ref = att.at[h, core, :, :, pl.ds(0, 2 * HD)]
        pltpu.make_async_copy(ref, ref, cross_recv.at[h]).wait()
        hand_copy(h, 0).start()
        hand_copy(h, 1).start()

    def pair_copy(h):
        ref = att.at[h, core]
        return remote(ref, ref, pair_send.at[h], pair_recv.at[h], device(x, y, z, twin))

    def pair(h):
        ref = att.at[h, core, :, :, pl.ds(0, 4 * HD)]
        pltpu.make_async_copy(ref, ref, att_recv.at[h]).wait()
        ref = att.at[h, core, :, :, pl.ds(0, 2 * HD)]
        pltpu.make_async_copy(ref, ref, hand_recv.at[h]).wait()
        pair_copy(h).start()

    def piece_copy(d, far):
        to = lax.rem(s + d, NS)
        bit = lax.rem(lax.div(to, 2), 2)
        bit = 1 - bit if far else bit
        k = 0 if far else 1
        src = held.at[last, lax.div(to, 4), bit, lax.rem(to, 2)]
        dst = att.at[last, core, bit, :, mine]
        if d == 0:
            return pltpu.make_async_copy(src, dst, last_recv.at[k])
        target = device(lax.div(to, 2), y, zbase + lax.rem(to, 2), core)
        return remote(src, dst, last_send.at[k * NS + d], last_recv.at[k], target)

    def last_pair_copy(far):
        ref = att.at[last, core, 1 - xbit if far else xbit]
        k = 0 if far else 1
        return remote(
            ref, ref, last_pair_send.at[k], last_pair_recv.at[k], device(x, y, z, twin)
        )

    def last_pair(far):
        k = 0 if far else 1
        ref = att.at[last, core, 1 - xbit if far else xbit]
        pltpu.make_async_copy(ref, ref, last_recv.at[k]).wait()
        last_pair_copy(far).start()

    def last_paired(far):
        k = 0 if far else 1
        ref = att.at[last, twin, 1 - xbit if far else xbit]
        pltpu.make_async_copy(ref, ref, last_pair_recv.at[k]).wait()

    quarter = (xbit * 2 + core) * QCOLS

    def term(h, bit, n):
        left = att[h, :, pl.ds(bit, 1)].reshape(2 * TOK, NS * HD)
        return jnp.dot(
            left, wbuf[h * NS * HD:(h + 1) * NS * HD, n * NCOL:(n + 1) * NCOL],
            preferred_element_type=jnp.float32,
        )

    def paired(h):
        ref = att.at[h, twin]
        pltpu.make_async_copy(ref, ref, pair_recv.at[h]).wait()

    def gather(h):
        paired(h)
        for far in (True, False):
            bit = 1 - xbit if far else xbit
            for n in range(QCOLS // NCOL):
                at = (0 if far else 1, slice(None), slice(n * NCOL, (n + 1) * NCOL))
                acc[at] = term(h, bit, n) if h == 0 else acc[at] + term(h, bit, n)

    z_step(1)
    relay(0)
    other(2)
    relay(1)
    z_step(2)
    attend(0)
    relay(2)
    attend(1)
    z_step(3)
    hand(0)
    relay(3)
    relay(4)
    attend(2)
    z_step(4)
    relay(5)
    relay(6)
    pair(0)
    hand(1)
    relay(7)
    pair(1)
    relayed()
    gather(0)
    gather(1)
    def ret_copy(n, blk, far):
        cols = pl.ds(n * NCOL, NCOL)
        to = pl.ds(pl.multiple_of(quarter + n * NCOL, NCOL), NCOL)
        src = prod.at[blk, (1 - xbit) if far else xbit, :, cols]
        dst = out_ref.at[:, to]
        k = (0 if blk is core else 1) + (0 if far else 2)
        if not far and blk is core:
            return pltpu.make_async_copy(src, dst, ret_recv.at[k * 3 + n])
        return remote(
            src, dst, ret_send.at[k * 3 + n], ret_recv.at[k * 3 + n],
            device(xother if far else x, y, z, blk),
        )

    for far in (True, False):
        bit = 1 - xbit if far else xbit
        last_pair(far)
        last_paired(far)
        for n in range(QCOLS // NCOL):
            total = acc[0 if far else 1, :, n * NCOL:(n + 1) * NCOL] + term(last, bit, n)
            prod[:, pl.ds(bit, 1), :, n * NCOL:(n + 1) * NCOL] = (
                total.astype(jnp.bfloat16).reshape(2, 1, TOK, NCOL)
            )
            for blk in (core, twin):
                ret_copy(n, blk, far).start()


    for n in range(QCOLS // NCOL):
        for far in (True, False):
            for blk in (core, twin):
                if far or blk is twin:
                    ret_copy(n, blk, far).wait_send()
        for far in (True, False):
            for blk in (core, twin):
                k = (0 if blk is core else 1) + (0 if far else 2)
                fq = ((1 - xbit if far else xbit) * 2 + blk) * QCOLS + n * NCOL
                ref = out_ref.at[:, pl.ds(pl.multiple_of(fq, NCOL), NCOL)]
                pltpu.make_async_copy(ref, ref, ret_recv.at[k * 3 + n]).wait()
    for k in range(NS):
        own = (x == k // 2) & (core == k % 2) & (zl == core)

        @pl.when(jnp.logical_not(own))
        def _():
            remote(
                wpad.at[:, pl.ds(0, QCOLS)], raw.at[s], first_send.at[k], first_recv.at[s],
                device(jnp.int32(k // 2), y, zbase + core, jnp.int32(k % 2)),
            ).wait_send()

    for h in range(NH):
        for d in range(1, NS):
            qkv_copy(h, d).wait_send()
    for h in range(last):
        for k in range(1, 4):
            own_copy(h, k).wait_send()
        for k in range(2):
            cross_copy(h, k).wait_send()
            hand_copy(h, k).wait_send()
        pair_copy(h).wait_send()
    for far in (True, False):
        for d in range(1, NS):
            piece_copy(d, far).wait_send()
        last_pair_copy(far).wait_send()
    for hops in range(4):
        z_copy(True, hops).wait_send()
        if hops < 3:
            z_copy(False, hops).wait_send()
    for i in range(8):
        for going_up in (True, False):
            y_copy(i, going_up).wait_send()
            relay_copy(i, going_up).wait_send()


def project(proj, w):
    bf = jnp.bfloat16
    dma = pltpu.SemaphoreType.DMA
    return pl.pallas_call(
        kernel,
        out_shape=jax.ShapeDtypeStruct((TOK, 4 * QCOLS), bf),
        in_specs=[pl.BlockSpec(memory_space=pl.ANY), pl.BlockSpec(memory_space=pl.ANY)],
        out_specs=pl.BlockSpec(memory_space=pltpu.VMEM),
        scratch_shapes=[
            pltpu.VMEM((NH, 3, NS * TOK, HD), bf),
            pltpu.VMEM((NH, 2, 2, 2, TOK, HD), bf),
            pltpu.VMEM((NH, 2, 2, TOK, NS * HD), bf),
            pltpu.VMEM((16, 4 * QCOLS), bf),
            pltpu.VMEM((NS, 16, QCOLS), bf),
            pltpu.VMEM((32 * ROWS, QCOLS), bf),
            pltpu.VMEM((2, 2, TOK, QCOLS), bf),
            dma((NS,)), dma((NS,)),
            dma((NH * NS,)), dma((NH,)),
            dma((7,)), dma((7,)),
            dma((16,)), dma((16,)),
            dma((16,)), dma((16,)),
            dma((NH * 4,)), dma((NH,)),
            dma((NH * 2,)), dma((NH,)),
            dma((NH * 2,)), dma((NH,)),
            dma((2 * NS,)), dma((2,)),
            dma((2,)), dma((2,)),
            dma((NH,)), dma((NH,)),
            dma((12,)), dma((12,)),
            pltpu.VMEM((12, 4 * QCOLS), bf), dma,
            pltpu.VMEM((2, 2 * TOK, QCOLS), jnp.float32),
        ],
        compiler_params=pltpu.CompilerParams(
            collective_id=0, has_side_effects=True, vmem_limit_bytes=62 << 20
        ),
        name="attend_project",
    )(proj, w)


def shards(projected, residual, timesteps, gate_table, out_weight):
    product = project(projected[0].transpose(1, 0, 2), out_weight)
    gate = lax.dynamic_slice(gate_table, (timesteps[0], 0), (1, gate_table.shape[1]))
    result = residual[0].astype(jnp.float32) + gate * product.astype(jnp.float32)
    return result.astype(jnp.bfloat16)[None]


def solution(mesh):
    placed = (
        P("tm", "seq", None, None),
        P("tm", "seq", None),
        P("tm"),
        P(),
        P(("tm", "seq"), None),
    )
    return jax.shard_map(
        shards, mesh=mesh, in_specs=placed, out_specs=P("tm", "seq", None), check_vma=False
    )
```

```python
import functools
import math

import jax
import jax.numpy as jnp
from jax import lax
from jax.experimental import pallas as pl
from jax.experimental.pallas import tpu as pltpu
from jax.sharding import PartitionSpec as P

MESH = pl.DeviceIdType.MESH
HD = 128
NH = 3
NS = 8
TOK = 128
QCOLS = 768
ROWS = 96
QBLK = 256
NCOL = 256


def coords():
    tm, s = lax.axis_index("tm"), lax.axis_index("seq")
    core = lax.rem(tm, 2)
    y = lax.rem(lax.div(tm, 2), 4)
    z = lax.div(tm, 8) * 2 + lax.rem(s, 2)
    return lax.div(s, 2), y, z, core


def device(x, y, z, core):
    return (lax.div(z, 2) * 8 + y * 2 + core, x * 2 + lax.rem(z, 2))


def kernel(
    proj, w_ref, out_ref,
    qkv, held, att, wpad, raw, wbuf, prod,
    first_send, first_recv, qkv_send, qkv_recv, z_send, z_recv, y_send, y_recv,
    relay_send, relay_recv, att_send, att_recv, cross_send, cross_recv, hand_send, hand_recv,
    last_send, last_recv, last_pair_send, last_pair_recv, pair_send, pair_recv, ret_send, ret_recv,
    wown, load_sem, acc,
):
    x, y, z, core = coords()
    s = lax.axis_index("seq")
    zl = lax.rem(z, 2)
    zbase = z - zl
    twin = 1 - core
    xbit = lax.rem(x, 2)
    xother = x + 1 - 2 * xbit
    up = lax.rem(y + 1, 4)
    down = lax.rem(y + 3, 4)
    zup = lax.rem(z + 1, 8)
    zdown = lax.rem(z + 7, 8)

    def remote(src, dst, send, recv, target):
        return pltpu.make_async_remote_copy(
            src_ref=src, dst_ref=dst, send_sem=send, recv_sem=recv,
            device_id=target, device_id_type=MESH,
        )

    barrier = pltpu.get_barrier_semaphore()
    peers = []
    for c in (core, twin):
        for d in range(NS):
            if c is core and d == 0:
                continue
            other = lax.rem(s + d, NS)
            peers.append(device(lax.div(other, 2), y, zbase + lax.rem(other, 2), c))
    zouter = lax.rem(z + 7 + 2 * zl, 8)
    peers.append(device(x, y, zouter, core))
    peers.append(device(x, up, z, core))
    peers.append(device(x, down, z, core))
    for peer in peers:
        pl.semaphore_signal(barrier, inc=1, device_id=peer, device_id_type=MESH)

    load = pltpu.make_async_copy(w_ref, wown, load_sem)
    load.start()
    wpad[...] = jnp.zeros_like(wpad)
    load.wait()
    wpad[0:12, :] = wown[...]
    pl.semaphore_wait(barrier, len(peers))

    for k in range(NS):
        xt, ct = k // 2, k % 2
        quarter = (xt % 2) * 2 + ct
        src = wpad.at[:, pl.ds(quarter * QCOLS, QCOLS)]
        own = (x == xt) & (core == ct) & (zl == core)

        @pl.when(own)
        def _():
            pltpu.make_async_copy(src, raw.at[s], first_recv.at[s]).start()

        @pl.when(jnp.logical_not(own))
        def _():
            remote(
                src, raw.at[s], first_send.at[k], first_recv.at[s],
                device(jnp.int32(xt), y, zbase + core, jnp.int32(ct)),
            ).start()

    def qkv_copy(h, d):
        other = lax.rem(s + d, NS)
        col = pl.multiple_of((NS * h + other) * HD, HD)
        src = proj.at[:, :, pl.ds(col, HD)]
        dst = qkv.at[h, :, pl.ds(pl.multiple_of(s * TOK, TOK), TOK), :]
        if d == 0:
            return pltpu.make_async_copy(src, dst, qkv_recv.at[h])
        target = device(lax.div(other, 2), y, zbase + lax.rem(other, 2), core)
        return remote(src, dst, qkv_send.at[h * NS + d], qkv_recv.at[h], target)

    def same(h):
        for d in (2, 6, 4, 0):
            qkv_copy(h, d).start()

    def other(h, some=(1, 7, 3, 5)):
        for d in some:
            qkv_copy(h, d).start()

    other(0)
    same(0)
    same(1)
    for k in range(NS):
        pltpu.make_async_copy(raw.at[k], raw.at[k], first_recv.at[k]).wait()
    row = lax.broadcasted_iota(jnp.int32, (ROWS, 128), 0)
    col = lax.broadcasted_iota(jnp.int32, (ROWS, 128), 1)
    piece = lax.div(row, 12)
    pick = (col == piece * 16 + (row - piece * 12)).astype(jnp.float32).astype(jnp.bfloat16)
    tile = jnp.dot(
        pick, raw[...].reshape(128, QCOLS), preferred_element_type=jnp.float32
    ).astype(jnp.bfloat16)

    def tile_row(ty, tz):
        return pl.multiple_of((lax.div(tz, 2) * 8 + ty * 2 + lax.rem(tz, 2)) * ROWS, 32)

    wbuf[pl.ds(tile_row(y, z), ROWS), :] = tile

    order = [0, -1, 1, -2, 2, -3, 3, -4]

    def slot(ty, off, lo=0, n=ROWS):
        first = tile_row(ty, lax.rem(z + off + 8, 8)) + lo
        return wbuf.at[pl.ds(pl.multiple_of(first, 16), n), :]

    def z_copy(going_up, hops):
        ref = slot(y, -hops if going_up else hops)
        k = (hops if going_up else 4 + hops)
        return remote(
            ref, ref, z_send.at[k], z_recv.at[k],
            device(x, y, zup if going_up else zdown, core),
        )

    def z_wait(going_up, hops):
        ref = slot(y, -(hops + 1) if going_up else hops + 1)
        k = (hops if going_up else 4 + hops)
        pltpu.make_async_copy(ref, ref, z_recv.at[k]).wait()

    def y_copy(i, going_up):
        ref = slot(y, order[i])
        k = 2 * i + (0 if going_up else 1)
        return remote(
            ref, ref, y_send.at[k], y_recv.at[k], device(x, up if going_up else down, z, core)
        )

    def relay_copy(i, going_up):
        ref = slot(down if going_up else up, order[i], 0 if going_up else 48, 48)
        k = 2 * i + (0 if going_up else 1)
        return remote(
            ref, ref, relay_send.at[k], relay_recv.at[k],
            device(x, up if going_up else down, z, core),
        )

    def share(i):
        y_copy(i, True).start()
        y_copy(i, False).start()

    def relay(*which):
        for i in which:
            for going_up in (True, False):
                ref = slot(down if going_up else up, order[i])
                k = 2 * i + (0 if going_up else 1)
                pltpu.make_async_copy(ref, ref, y_recv.at[k]).wait()
                relay_copy(i, going_up).start()

    def relayed():
        for i in range(8):
            for going_up in (True, False):
                ref = slot(lax.rem(y + 2, 4), order[i], 0 if going_up else 48, 48)
                k = 2 * i + (0 if going_up else 1)
                pltpu.make_async_copy(ref, ref, relay_recv.at[k]).wait()

    def z_step(hops):
        z_wait(True, hops - 1)
        if hops < 4:
            z_copy(True, hops).start()
        share(2 * hops - 1)
        if hops < 4:
            z_wait(False, hops - 1)
            if hops < 3:
                z_copy(False, hops).start()
            share(2 * hops)

    def z_first():
        z_copy(True, 0).start()
        z_copy(False, 0).start()
        share(0)

    z_first()
    other(1)
    same(2)

    last = NH - 1

    def attend(h):
        ref = qkv.at[h]
        pltpu.make_async_copy(ref, ref, qkv_recv.at[h]).wait()
        factor = math.log2(math.e) / math.sqrt(HD)

        @pl.loop(0, NS * TOK // QBLK)
        def _(i):
            q = qkv[h, 0, pl.ds(pl.multiple_of(i * QBLK, QBLK), QBLK), :]
            scores = lax.dot_general(
                q, qkv[h, 1], (((1,), (1,)), ((), ())), preferred_element_type=jnp.float32
            ) * factor
            weights = jnp.exp2(scores - jnp.max(scores, axis=1, keepdims=True))
            totals = jnp.sum(weights, axis=1, keepdims=True)
            summed = jnp.dot(
                weights.astype(jnp.bfloat16), qkv[h, 2], preferred_element_type=jnp.float32
            )
            res = (summed / totals).astype(jnp.bfloat16).reshape(1, 1, 2, TOK, HD)
            held[pl.ds(h, 1), pl.ds(lax.div(i, 2), 1), pl.ds(lax.rem(i, 2), 1)] = res[None]

        if h < last:
            for k in (0, 1):
                cross_copy(h, k).start()
            for k in (1, 3, 2, 0):
                own_copy(h, k).start()
        else:
            for far in (True, False):
                for d in (1, 7, 3, 5, 2, 6, 4, 0):
                    piece_copy(d, far).start()

    mine = pl.ds(pl.multiple_of(s * HD, HD), HD)

    def own_copy(h, k):
        xt = lax.rem(x + k, 4)
        src = held.at[h, lax.div(xt, 2), :, zl]
        dst = att.at[h, core, :, :, mine]
        if k == 0:
            return pltpu.make_async_copy(src, dst, att_recv.at[h])
        return remote(src, dst, att_send.at[h * 4 + k], att_recv.at[h], device(xt, y, z, core))

    def cross_copy(h, k):
        xt = x if k == 0 else 3 - x
        src = held.at[h, lax.div(xt, 2), :, 1 - zl]
        dst = att.at[h, core, :, :, mine]
        return remote(
            src, dst, cross_send.at[h * 2 + k], cross_recv.at[h],
            device(xt, y, zbase + 1 - zl, core),
        )

    def hand_copy(h, k):
        xt = x if k == 0 else 3 - x
        cols = pl.ds(pl.multiple_of((xt * 2 + 1 - zl) * HD, HD), HD)
        ref = att.at[h, core, :, :, cols]
        return remote(
            ref, ref, hand_send.at[h * 2 + k], hand_recv.at[h], device(xother, y, z, core)
        )

    def hand(h):
        ref = att.at[h, core, :, :, pl.ds(0, 2 * HD)]
        pltpu.make_async_copy(ref, ref, cross_recv.at[h]).wait()
        hand_copy(h, 0).start()
        hand_copy(h, 1).start()

    def pair_copy(h):
        ref = att.at[h, core]
        return remote(ref, ref, pair_send.at[h], pair_recv.at[h], device(x, y, z, twin))

    def pair(h):
        ref = att.at[h, core, :, :, pl.ds(0, 4 * HD)]
        pltpu.make_async_copy(ref, ref, att_recv.at[h]).wait()
        ref = att.at[h, core, :, :, pl.ds(0, 2 * HD)]
        pltpu.make_async_copy(ref, ref, hand_recv.at[h]).wait()
        pair_copy(h).start()

    def piece_copy(d, far):
        to = lax.rem(s + d, NS)
        bit = lax.rem(lax.div(to, 2), 2)
        bit = 1 - bit if far else bit
        k = 0 if far else 1
        src = held.at[last, lax.div(to, 4), bit, lax.rem(to, 2)]
        dst = att.at[last, core, bit, :, mine]
        if d == 0:
            return pltpu.make_async_copy(src, dst, last_recv.at[k])
        target = device(lax.div(to, 2), y, zbase + lax.rem(to, 2), core)
        return remote(src, dst, last_send.at[k * NS + d], last_recv.at[k], target)

    def last_pair_copy(far):
        ref = att.at[last, core, 1 - xbit if far else xbit]
        k = 0 if far else 1
        return remote(
            ref, ref, last_pair_send.at[k], last_pair_recv.at[k], device(x, y, z, twin)
        )

    def last_pair(far):
        k = 0 if far else 1
        ref = att.at[last, core, 1 - xbit if far else xbit]
        pltpu.make_async_copy(ref, ref, last_recv.at[k]).wait()
        last_pair_copy(far).start()

    def last_paired(far):
        k = 0 if far else 1
        ref = att.at[last, twin, 1 - xbit if far else xbit]
        pltpu.make_async_copy(ref, ref, last_pair_recv.at[k]).wait()

    quarter = (xbit * 2 + core) * QCOLS

    def term(h, bit, n):
        left = att[h, :, pl.ds(bit, 1)].reshape(2 * TOK, NS * HD)
        return jnp.dot(
            left, wbuf[h * NS * HD:(h + 1) * NS * HD, n * NCOL:(n + 1) * NCOL],
            preferred_element_type=jnp.float32,
        )

    def paired(h):
        ref = att.at[h, twin]
        pltpu.make_async_copy(ref, ref, pair_recv.at[h]).wait()

    def gather(h):
        paired(h)
        for far in (True, False):
            bit = 1 - xbit if far else xbit
            for n in range(QCOLS // NCOL):
                at = (0 if far else 1, slice(None), slice(n * NCOL, (n + 1) * NCOL))
                acc[at] = term(h, bit, n) if h == 0 else acc[at] + term(h, bit, n)

    z_step(1)
    relay(0)
    other(2)
    relay(1)
    z_step(2)
    attend(0)
    relay(2)
    attend(1)
    relay(3)
    relay(4)
    z_step(3)
    attend(2)
    hand(0)
    z_step(4)
    relay(5)
    hand(1)
    relay(6)
    pair(0)
    relay(7)
    pair(1)
    relayed()
    gather(0)
    gather(1)
    def ret_copy(n, blk, far):
        cols = pl.ds(n * NCOL, NCOL)
        to = pl.ds(pl.multiple_of(quarter + n * NCOL, NCOL), NCOL)
        src = prod.at[blk, (1 - xbit) if far else xbit, :, cols]
        dst = out_ref.at[:, to]
        k = (0 if blk is core else 1) + (0 if far else 2)
        if not far and blk is core:
            return pltpu.make_async_copy(src, dst, ret_recv.at[k * 3 + n])
        return remote(
            src, dst, ret_send.at[k * 3 + n], ret_recv.at[k * 3 + n],
            device(xother if far else x, y, z, blk),
        )

    for far in (True, False):
        bit = 1 - xbit if far else xbit
        last_pair(far)
        last_paired(far)
        for n in range(QCOLS // NCOL):
            total = acc[0 if far else 1, :, n * NCOL:(n + 1) * NCOL] + term(last, bit, n)
            prod[:, pl.ds(bit, 1), :, n * NCOL:(n + 1) * NCOL] = (
                total.astype(jnp.bfloat16).reshape(2, 1, TOK, NCOL)
            )
            for blk in (core, twin):
                ret_copy(n, blk, far).start()


    for n in range(QCOLS // NCOL):
        for far in (True, False):
            for blk in (core, twin):
                if far or blk is twin:
                    ret_copy(n, blk, far).wait_send()
        for far in (True, False):
            for blk in (core, twin):
                k = (0 if blk is core else 1) + (0 if far else 2)
                fq = ((1 - xbit if far else xbit) * 2 + blk) * QCOLS + n * NCOL
                ref = out_ref.at[:, pl.ds(pl.multiple_of(fq, NCOL), NCOL)]
                pltpu.make_async_copy(ref, ref, ret_recv.at[k * 3 + n]).wait()
    for k in range(NS):
        own = (x == k // 2) & (core == k % 2) & (zl == core)

        @pl.when(jnp.logical_not(own))
        def _():
            remote(
                wpad.at[:, pl.ds(0, QCOLS)], raw.at[s], first_send.at[k], first_recv.at[s],
                device(jnp.int32(k // 2), y, zbase + core, jnp.int32(k % 2)),
            ).wait_send()

    for h in range(NH):
        for d in range(1, NS):
            qkv_copy(h, d).wait_send()
    for h in range(last):
        for k in range(1, 4):
            own_copy(h, k).wait_send()
        for k in range(2):
            cross_copy(h, k).wait_send()
            hand_copy(h, k).wait_send()
        pair_copy(h).wait_send()
    for far in (True, False):
        for d in range(1, NS):
            piece_copy(d, far).wait_send()
        last_pair_copy(far).wait_send()
    for hops in range(4):
        z_copy(True, hops).wait_send()
        if hops < 3:
            z_copy(False, hops).wait_send()
    for i in range(8):
        for going_up in (True, False):
            y_copy(i, going_up).wait_send()
            relay_copy(i, going_up).wait_send()


def project(proj, w):
    bf = jnp.bfloat16
    dma = pltpu.SemaphoreType.DMA
    return pl.pallas_call(
        kernel,
        out_shape=jax.ShapeDtypeStruct((TOK, 4 * QCOLS), bf),
        in_specs=[pl.BlockSpec(memory_space=pl.ANY), pl.BlockSpec(memory_space=pl.ANY)],
        out_specs=pl.BlockSpec(memory_space=pltpu.VMEM),
        scratch_shapes=[
            pltpu.VMEM((NH, 3, NS * TOK, HD), bf),
            pltpu.VMEM((NH, 2, 2, 2, TOK, HD), bf),
            pltpu.VMEM((NH, 2, 2, TOK, NS * HD), bf),
            pltpu.VMEM((16, 4 * QCOLS), bf),
            pltpu.VMEM((NS, 16, QCOLS), bf),
            pltpu.VMEM((32 * ROWS, QCOLS), bf),
            pltpu.VMEM((2, 2, TOK, QCOLS), bf),
            dma((NS,)), dma((NS,)),
            dma((NH * NS,)), dma((NH,)),
            dma((7,)), dma((7,)),
            dma((16,)), dma((16,)),
            dma((16,)), dma((16,)),
            dma((NH * 4,)), dma((NH,)),
            dma((NH * 2,)), dma((NH,)),
            dma((NH * 2,)), dma((NH,)),
            dma((2 * NS,)), dma((2,)),
            dma((2,)), dma((2,)),
            dma((NH,)), dma((NH,)),
            dma((12,)), dma((12,)),
            pltpu.VMEM((12, 4 * QCOLS), bf), dma,
            pltpu.VMEM((2, 2 * TOK, QCOLS), jnp.float32),
        ],
        compiler_params=pltpu.CompilerParams(
            collective_id=0, has_side_effects=True, vmem_limit_bytes=53 << 20
        ),
        name="attend_project",
    )(proj, w)


def shards(projected, residual, timesteps, gate_table, out_weight):
    product = project(projected[0].transpose(1, 0, 2), out_weight)
    gate = lax.dynamic_slice(gate_table, (timesteps[0], 0), (1, gate_table.shape[1]))
    result = residual[0].astype(jnp.float32) + gate * product.astype(jnp.float32)
    return result.astype(jnp.bfloat16)[None]


def solution(mesh):
    placed = (
        P("tm", "seq", None, None),
        P("tm", "seq", None),
        P("tm"),
        P(),
        P(("tm", "seq"), None),
    )
    return jax.shard_map(
        shards, mesh=mesh, in_specs=placed, out_specs=P("tm", "seq", None), check_vma=False
    )
```

```python
import functools
import math

import jax
import jax.numpy as jnp
from jax import lax
from jax.experimental import pallas as pl
from jax.experimental.pallas import tpu as pltpu
from jax.sharding import PartitionSpec as P

MESH = pl.DeviceIdType.MESH
HD = 128
NH = 3
NS = 8
TOK = 128
QCOLS = 768
ROWS = 96
QBLK = 256
NCOL = 256


def coords():
    tm, s = lax.axis_index("tm"), lax.axis_index("seq")
    core = lax.rem(tm, 2)
    y = lax.rem(lax.div(tm, 2), 4)
    z = lax.div(tm, 8) * 2 + lax.rem(s, 2)
    return lax.div(s, 2), y, z, core


def device(x, y, z, core):
    return (lax.div(z, 2) * 8 + y * 2 + core, x * 2 + lax.rem(z, 2))


def kernel(
    proj, w_ref, out_ref,
    qkv, held, att, wpad, raw, wbuf, prod,
    first_send, first_recv, qkv_send, qkv_recv, z_send, z_recv, y_send, y_recv,
    relay_send, relay_recv, att_send, att_recv, cross_send, cross_recv, hand_send, hand_recv,
    last_send, last_recv, last_pair_send, last_pair_recv, pair_send, pair_recv, ret_send, ret_recv,
    wown, load_sem, acc,
):
    x, y, z, core = coords()
    s = lax.axis_index("seq")
    zl = lax.rem(z, 2)
    zbase = z - zl
    twin = 1 - core
    xbit = lax.rem(x, 2)
    xother = x + 1 - 2 * xbit
    up = lax.rem(y + 1, 4)
    down = lax.rem(y + 3, 4)
    zup = lax.rem(z + 1, 8)
    zdown = lax.rem(z + 7, 8)

    def remote(src, dst, send, recv, target):
        return pltpu.make_async_remote_copy(
            src_ref=src, dst_ref=dst, send_sem=send, recv_sem=recv,
            device_id=target, device_id_type=MESH,
        )

    barrier = pltpu.get_barrier_semaphore()
    peers = []
    for c in (core, twin):
        for d in range(NS):
            if c is core and d == 0:
                continue
            other = lax.rem(s + d, NS)
            peers.append(device(lax.div(other, 2), y, zbase + lax.rem(other, 2), c))
    zouter = lax.rem(z + 7 + 2 * zl, 8)
    peers.append(device(x, y, zouter, core))
    peers.append(device(x, up, z, core))
    peers.append(device(x, down, z, core))
    for peer in peers:
        pl.semaphore_signal(barrier, inc=1, device_id=peer, device_id_type=MESH)

    load = pltpu.make_async_copy(w_ref, wown, load_sem)
    load.start()
    wpad[...] = jnp.zeros_like(wpad)
    load.wait()
    wpad[0:12, :] = wown[...]
    pl.semaphore_wait(barrier, len(peers))

    for k in range(NS):
        xt, ct = k // 2, k % 2
        quarter = (xt % 2) * 2 + ct
        src = wpad.at[:, pl.ds(quarter * QCOLS, QCOLS)]
        own = (x == xt) & (core == ct) & (zl == core)

        @pl.when(own)
        def _():
            pltpu.make_async_copy(src, raw.at[s], first_recv.at[s]).start()

        @pl.when(jnp.logical_not(own))
        def _():
            remote(
                src, raw.at[s], first_send.at[k], first_recv.at[s],
                device(jnp.int32(xt), y, zbase + core, jnp.int32(ct)),
            ).start()

    def qkv_copy(h, d):
        other = lax.rem(s + d, NS)
        col = pl.multiple_of((NS * h + other) * HD, HD)
        src = proj.at[:, :, pl.ds(col, HD)]
        dst = qkv.at[h, :, pl.ds(pl.multiple_of(s * TOK, TOK), TOK), :]
        if d == 0:
            return pltpu.make_async_copy(src, dst, qkv_recv.at[h])
        target = device(lax.div(other, 2), y, zbase + lax.rem(other, 2), core)
        return remote(src, dst, qkv_send.at[h * NS + d], qkv_recv.at[h], target)

    def same(h):
        for d in (2, 6, 4, 0):
            qkv_copy(h, d).start()

    def other(h, some=(1, 7, 3, 5)):
        for d in some:
            qkv_copy(h, d).start()

    other(0)
    same(0)
    same(1)
    for k in range(NS):
        pltpu.make_async_copy(raw.at[k], raw.at[k], first_recv.at[k]).wait()
    row = lax.broadcasted_iota(jnp.int32, (ROWS, 128), 0)
    col = lax.broadcasted_iota(jnp.int32, (ROWS, 128), 1)
    piece = lax.div(row, 12)
    pick = (col == piece * 16 + (row - piece * 12)).astype(jnp.float32).astype(jnp.bfloat16)
    tile = jnp.dot(
        pick, raw[...].reshape(128, QCOLS), preferred_element_type=jnp.float32
    ).astype(jnp.bfloat16)

    def tile_row(ty, tz):
        return pl.multiple_of((lax.div(tz, 2) * 8 + ty * 2 + lax.rem(tz, 2)) * ROWS, 32)

    wbuf[pl.ds(tile_row(y, z), ROWS), :] = tile

    order = [0, -1, 1, -2, 2, -3, 3, -4]

    def slot(ty, off, lo=0, n=ROWS):
        first = tile_row(ty, lax.rem(z + off + 8, 8)) + lo
        return wbuf.at[pl.ds(pl.multiple_of(first, 16), n), :]

    def z_copy(going_up, hops):
        ref = slot(y, -hops if going_up else hops)
        k = (hops if going_up else 4 + hops)
        return remote(
            ref, ref, z_send.at[k], z_recv.at[k],
            device(x, y, zup if going_up else zdown, core),
        )

    def z_wait(going_up, hops):
        ref = slot(y, -(hops + 1) if going_up else hops + 1)
        k = (hops if going_up else 4 + hops)
        pltpu.make_async_copy(ref, ref, z_recv.at[k]).wait()

    def y_copy(i, going_up):
        ref = slot(y, order[i])
        k = 2 * i + (0 if going_up else 1)
        return remote(
            ref, ref, y_send.at[k], y_recv.at[k], device(x, up if going_up else down, z, core)
        )

    def relay_copy(i, going_up):
        ref = slot(down if going_up else up, order[i], 0 if going_up else 48, 48)
        k = 2 * i + (0 if going_up else 1)
        return remote(
            ref, ref, relay_send.at[k], relay_recv.at[k],
            device(x, up if going_up else down, z, core),
        )

    def share(i):
        y_copy(i, True).start()
        y_copy(i, False).start()

    def relay(*which):
        for i in which:
            for going_up in (True, False):
                ref = slot(down if going_up else up, order[i])
                k = 2 * i + (0 if going_up else 1)
                pltpu.make_async_copy(ref, ref, y_recv.at[k]).wait()
                relay_copy(i, going_up).start()

    def relayed():
        for i in range(8):
            for going_up in (True, False):
                ref = slot(lax.rem(y + 2, 4), order[i], 0 if going_up else 48, 48)
                k = 2 * i + (0 if going_up else 1)
                pltpu.make_async_copy(ref, ref, relay_recv.at[k]).wait()

    def z_step(hops):
        z_wait(True, hops - 1)
        if hops < 4:
            z_copy(True, hops).start()
        share(2 * hops - 1)
        if hops < 4:
            z_wait(False, hops - 1)
            if hops < 3:
                z_copy(False, hops).start()
            share(2 * hops)

    def z_first():
        z_copy(True, 0).start()
        z_copy(False, 0).start()
        share(0)

    z_first()
    other(1)
    same(2)

    last = NH - 1

    def attend(h):
        ref = qkv.at[h]
        pltpu.make_async_copy(ref, ref, qkv_recv.at[h]).wait()
        factor = math.log2(math.e) / math.sqrt(HD)

        @pl.loop(0, NS * TOK // QBLK)
        def _(i):
            q = qkv[h, 0, pl.ds(pl.multiple_of(i * QBLK, QBLK), QBLK), :]
            scores = lax.dot_general(
                q, qkv[h, 1], (((1,), (1,)), ((), ())), preferred_element_type=jnp.float32
            ) * factor
            weights = jnp.exp2(scores - jnp.max(scores, axis=1, keepdims=True))
            totals = jnp.sum(weights, axis=1, keepdims=True)
            summed = jnp.dot(
                weights.astype(jnp.bfloat16), qkv[h, 2], preferred_element_type=jnp.float32
            )
            res = (summed / totals).astype(jnp.bfloat16).reshape(1, 1, 2, TOK, HD)
            held[pl.ds(h, 1), pl.ds(lax.div(i, 2), 1), pl.ds(lax.rem(i, 2), 1)] = res[None]

        if h < last:
            for k in (0, 1):
                cross_copy(h, k).start()
            for k in (1, 3, 2, 0):
                own_copy(h, k).start()
        else:
            for far in (True, False):
                for d in (1, 7, 3, 5, 2, 6, 4, 0):
                    piece_copy(d, far).start()

    mine = pl.ds(pl.multiple_of(s * HD, HD), HD)

    def own_copy(h, k):
        xt = lax.rem(x + k, 4)
        src = held.at[h, lax.div(xt, 2), :, zl]
        dst = att.at[h, core, :, :, mine]
        if k == 0:
            return pltpu.make_async_copy(src, dst, att_recv.at[h])
        return remote(src, dst, att_send.at[h * 4 + k], att_recv.at[h], device(xt, y, z, core))

    def cross_copy(h, k):
        xt = x if k == 0 else 3 - x
        src = held.at[h, lax.div(xt, 2), :, 1 - zl]
        dst = att.at[h, core, :, :, mine]
        return remote(
            src, dst, cross_send.at[h * 2 + k], cross_recv.at[h],
            device(xt, y, zbase + 1 - zl, core),
        )

    def hand_copy(h, k):
        xt = x if k == 0 else 3 - x
        cols = pl.ds(pl.multiple_of((xt * 2 + 1 - zl) * HD, HD), HD)
        ref = att.at[h, core, :, :, cols]
        return remote(
            ref, ref, hand_send.at[h * 2 + k], hand_recv.at[h], device(xother, y, z, core)
        )

    def hand(h):
        ref = att.at[h, core, :, :, pl.ds(0, 2 * HD)]
        pltpu.make_async_copy(ref, ref, cross_recv.at[h]).wait()
        hand_copy(h, 0).start()
        hand_copy(h, 1).start()

    def pair_copy(h):
        ref = att.at[h, core]
        return remote(ref, ref, pair_send.at[h], pair_recv.at[h], device(x, y, z, twin))

    def pair(h):
        ref = att.at[h, core, :, :, pl.ds(0, 4 * HD)]
        pltpu.make_async_copy(ref, ref, att_recv.at[h]).wait()
        ref = att.at[h, core, :, :, pl.ds(0, 2 * HD)]
        pltpu.make_async_copy(ref, ref, hand_recv.at[h]).wait()
        pair_copy(h).start()

    def piece_copy(d, far):
        to = lax.rem(s + d, NS)
        bit = lax.rem(lax.div(to, 2), 2)
        bit = 1 - bit if far else bit
        k = 0 if far else 1
        src = held.at[last, lax.div(to, 4), bit, lax.rem(to, 2)]
        dst = att.at[last, core, bit, :, mine]
        if d == 0:
            return pltpu.make_async_copy(src, dst, last_recv.at[k])
        target = device(lax.div(to, 2), y, zbase + lax.rem(to, 2), core)
        return remote(src, dst, last_send.at[k * NS + d], last_recv.at[k], target)

    def last_pair_copy(far):
        ref = att.at[last, core, 1 - xbit if far else xbit]
        k = 0 if far else 1
        return remote(
            ref, ref, last_pair_send.at[k], last_pair_recv.at[k], device(x, y, z, twin)
        )

    def last_pair(far):
        k = 0 if far else 1
        ref = att.at[last, core, 1 - xbit if far else xbit]
        pltpu.make_async_copy(ref, ref, last_recv.at[k]).wait()
        last_pair_copy(far).start()

    def last_paired(far):
        k = 0 if far else 1
        ref = att.at[last, twin, 1 - xbit if far else xbit]
        pltpu.make_async_copy(ref, ref, last_pair_recv.at[k]).wait()

    quarter = (xbit * 2 + core) * QCOLS

    def term(h, bit, n):
        left = att[h, :, pl.ds(bit, 1)].reshape(2 * TOK, NS * HD)
        return jnp.dot(
            left, wbuf[h * NS * HD:(h + 1) * NS * HD, n * NCOL:(n + 1) * NCOL],
            preferred_element_type=jnp.float32,
        )

    def paired(h):
        ref = att.at[h, twin]
        pltpu.make_async_copy(ref, ref, pair_recv.at[h]).wait()

    def gather(h):
        paired(h)
        for n in range(QCOLS // NCOL):
            at = (slice(None), slice(n * NCOL, (n + 1) * NCOL))
            acc[at] = term(h, 1 - xbit, n) if h == 0 else acc[at] + term(h, 1 - xbit, n)

    z_step(1)
    relay(0)
    other(2)
    relay(1)
    z_step(2)
    attend(0)
    relay(2)
    attend(1)
    relay(3)
    relay(4)
    z_step(3)
    attend(2)
    hand(0)
    z_step(4)
    relay(5)
    hand(1)
    relay(6)
    pair(0)
    relay(7)
    pair(1)
    relayed()
    gather(0)
    gather(1)
    def ret_copy(n, blk, far):
        cols = pl.ds(n * NCOL, NCOL)
        to = pl.ds(pl.multiple_of(quarter + n * NCOL, NCOL), NCOL)
        src = prod.at[blk, (1 - xbit) if far else xbit, :, cols]
        dst = out_ref.at[:, to]
        k = (0 if blk is core else 1) + (0 if far else 2)
        if not far and blk is core:
            return pltpu.make_async_copy(src, dst, ret_recv.at[k * 3 + n])
        return remote(
            src, dst, ret_send.at[k * 3 + n], ret_recv.at[k * 3 + n],
            device(xother if far else x, y, z, blk),
        )

    for far in (True, False):
        bit = 1 - xbit if far else xbit
        last_pair(far)
        last_paired(far)
        for n in range(QCOLS // NCOL):
            if far:
                total = acc[:, n * NCOL:(n + 1) * NCOL]
            else:
                total = term(0, bit, n) + term(1, bit, n)
            total = total + term(last, bit, n)
            prod[:, pl.ds(bit, 1), :, n * NCOL:(n + 1) * NCOL] = (
                total.astype(jnp.bfloat16).reshape(2, 1, TOK, NCOL)
            )
            for blk in (core, twin):
                ret_copy(n, blk, far).start()


    for n in range(QCOLS // NCOL):
        for far in (True, False):
            for blk in (core, twin):
                if far or blk is twin:
                    ret_copy(n, blk, far).wait_send()
        for far in (True, False):
            for blk in (core, twin):
                k = (0 if blk is core else 1) + (0 if far else 2)
                fq = ((1 - xbit if far else xbit) * 2 + blk) * QCOLS + n * NCOL
                ref = out_ref.at[:, pl.ds(pl.multiple_of(fq, NCOL), NCOL)]
                pltpu.make_async_copy(ref, ref, ret_recv.at[k * 3 + n]).wait()
    for k in range(NS):
        own = (x == k // 2) & (core == k % 2) & (zl == core)

        @pl.when(jnp.logical_not(own))
        def _():
            remote(
                wpad.at[:, pl.ds(0, QCOLS)], raw.at[s], first_send.at[k], first_recv.at[s],
                device(jnp.int32(k // 2), y, zbase + core, jnp.int32(k % 2)),
            ).wait_send()

    for h in range(NH):
        for d in range(1, NS):
            qkv_copy(h, d).wait_send()
    for h in range(last):
        for k in range(1, 4):
            own_copy(h, k).wait_send()
        for k in range(2):
            cross_copy(h, k).wait_send()
            hand_copy(h, k).wait_send()
        pair_copy(h).wait_send()
    for far in (True, False):
        for d in range(1, NS):
            piece_copy(d, far).wait_send()
        last_pair_copy(far).wait_send()
    for hops in range(4):
        z_copy(True, hops).wait_send()
        if hops < 3:
            z_copy(False, hops).wait_send()
    for i in range(8):
        for going_up in (True, False):
            y_copy(i, going_up).wait_send()
            relay_copy(i, going_up).wait_send()


def project(proj, w):
    bf = jnp.bfloat16
    dma = pltpu.SemaphoreType.DMA
    return pl.pallas_call(
        kernel,
        out_shape=jax.ShapeDtypeStruct((TOK, 4 * QCOLS), bf),
        in_specs=[pl.BlockSpec(memory_space=pl.ANY), pl.BlockSpec(memory_space=pl.ANY)],
        out_specs=pl.BlockSpec(memory_space=pltpu.VMEM),
        scratch_shapes=[
            pltpu.VMEM((NH, 3, NS * TOK, HD), bf),
            pltpu.VMEM((NH, 2, 2, 2, TOK, HD), bf),
            pltpu.VMEM((NH, 2, 2, TOK, NS * HD), bf),
            pltpu.VMEM((16, 4 * QCOLS), bf),
            pltpu.VMEM((NS, 16, QCOLS), bf),
            pltpu.VMEM((32 * ROWS, QCOLS), bf),
            pltpu.VMEM((2, 2, TOK, QCOLS), bf),
            dma((NS,)), dma((NS,)),
            dma((NH * NS,)), dma((NH,)),
            dma((7,)), dma((7,)),
            dma((16,)), dma((16,)),
            dma((16,)), dma((16,)),
            dma((NH * 4,)), dma((NH,)),
            dma((NH * 2,)), dma((NH,)),
            dma((NH * 2,)), dma((NH,)),
            dma((2 * NS,)), dma((2,)),
            dma((2,)), dma((2,)),
            dma((NH,)), dma((NH,)),
            dma((12,)), dma((12,)),
            pltpu.VMEM((12, 4 * QCOLS), bf), dma,
            pltpu.VMEM((2 * TOK, QCOLS), jnp.float32),
        ],
        compiler_params=pltpu.CompilerParams(
            collective_id=0, has_side_effects=True, vmem_limit_bytes=53 << 20
        ),
        name="attend_project",
    )(proj, w)


def shards(projected, residual, timesteps, gate_table, out_weight):
    product = project(projected[0].transpose(1, 0, 2), out_weight)
    gate = lax.dynamic_slice(gate_table, (timesteps[0], 0), (1, gate_table.shape[1]))
    result = residual[0].astype(jnp.float32) + gate * product.astype(jnp.float32)
    return result.astype(jnp.bfloat16)[None]


def solution(mesh):
    placed = (
        P("tm", "seq", None, None),
        P("tm", "seq", None),
        P("tm"),
        P(),
        P(("tm", "seq"), None),
    )
    return jax.shard_map(
        shards, mesh=mesh, in_specs=placed, out_specs=P("tm", "seq", None), check_vma=False
    )
```
